32 devices in a mesh: pipe: 2 (over y), ctx: 8 (over z, x), tp: 2 (over core).
Axes of the slice: x: 2, y: 2, z: 4, core: 2. Of those that a mesh axis runs over, the one named last changes fastest.
Arguments:
- inputs: bfloat16 [2, 1024, 1536], P(None, ('ctx', 'tp')), may hold values from -6 to 6
- cotangent: bfloat16 [2, 1024, 1536], P(None, ('ctx', 'tp')), may hold values from -6 to 6
- norm_attn: float32 [2, 1536], P('pipe'), may hold values from 0.1 to 1.9
- w_query: bfloat16 [2, 1536, 1536], P('pipe', None, 'tp'), may hold values from -0.15625 to 0.15625
- w_key: bfloat16 [2, 1536, 768], P('pipe', None, 'tp'), may hold values from -0.15625 to 0.15625
- w_value: bfloat16 [2, 1536, 768], P('pipe', None, 'tp'), may hold values from -0.15625 to 0.15625
- w_out: bfloat16 [2, 1536, 1536], P('pipe', None, 'tp'), may hold values from -2 to 2
- norm_mlp: float32 [2, 1536], P('pipe'), may hold values from 0.1 to 1.9
- w_gate: bfloat16 [2, 1536, 4096], P('pipe', None, 'tp'), may hold values from -0.15625 to 0.15625
- w_up: bfloat16 [2, 1536, 4096], P('pipe', None, 'tp'), may hold values from -0.15625 to 0.15625
- w_down: bfloat16 [2, 1536, 4096], P('pipe', None, 'tp'), may hold values from -0.09375 to 0.09375
Outputs:
- section_outputs: bfloat16 [2, 2, 1024, 1536], P('pipe', None, ('ctx', 'tp'))
- input_grads: float32 [2, 2, 1024, 1536], P('pipe', None, ('ctx', 'tp'))
- grad_norm_attn: float32 [2, 1536], P('pipe', 'ctx')
- grad_query: float32 [2, 1536, 1536], P('pipe', 'ctx', 'tp')
- grad_key: float32 [2, 1536, 768], P('pipe', 'ctx', 'tp')
- grad_value: float32 [2, 1536, 768], P('pipe', 'ctx', 'tp')
- grad_out: float32 [2, 1536, 1536], P('pipe', 'ctx', 'tp')
- grad_norm_mlp: float32 [2, 1536], P('pipe', 'ctx')
- grad_gate: float32 [2, 1536, 4096], P('pipe', 'ctx', 'tp')
- grad_up: float32 [2, 1536, 4096], P('pipe', 'ctx', 'tp')
- grad_down: float32 [2, 1536, 4096], P('pipe', 'ctx', 'tp')
The draws below stay inside these ranges and needn't reach their ends.
All inputs are finite; a program needn't handle non-finite values.
Results may differ from the reference program's by a relative error of at most 0.03.
Values may be sent and summed in bfloat16 or wider, within the bound.
No kernel may reach another device: no remote copies, remote signals or barrier semaphores. Data moves between devices by JAX's collectives and lax.ppermute only.
A program may use at most 256 MiB of HBM per device.

```python
import math
import jax
import jax.numpy as jnp
from jax import lax

D = 1536
H = 16
KV = 8
HD = 96
FF = 4096
SPAN = 128
MB = 2
LAYERS = 2
SEQ = 1024


def strengthened(values, stream_key, source, target, blocks, factor):
    def block_of(position):
        return (jnp.arange(values.shape[position]) // (values.shape[position] // blocks)).reshape((-1,) + (1,) * (values.ndim - 1 - position))

    near = jax.random.permutation(stream_key, blocks)[block_of(target)]
    far = (block_of(target) + blocks // 2) % blocks
    return jnp.where((block_of(source) == near) | (block_of(source) == far), factor * values, values)


def steps_of(rng, shape, split, smallest, top_value):
    def one(axis_at, blocks):
        draws = jax.random.uniform(jax.random.fold_in(jax.random.fold_in(rng, 6), axis_at), (blocks,), jnp.float32, smallest / len(split), top_value / len(split))
        return jnp.repeat(jnp.exp(draws), shape[axis_at] // blocks).reshape((-1,) + (1,) * (len(shape) - axis_at - 1))

    factor_of = one(*split[0])
    for cut in split[1:]:
        factor_of = factor_of * one(*cut)
    return factor_of


def noise(own_key, extent, deviation, limit, cuts=(), held_as=jnp.bfloat16):
    array = jax.random.normal(own_key, extent, jnp.float32) * deviation
    if len(cuts) > 0:
        array = steps_of(own_key, extent, cuts, -0.22, 0.18) * array
    return jnp.clip(array, min=-limit, max=limit).astype(held_as)


def gaussian_with(key, dims, deviation, reach, shards, heavy, held_as=jnp.bfloat16):
    values = deviation * jax.random.normal(key, dims, jnp.float32)
    if shards:
        values = values * steps_of(key, dims, shards, -0.22, 0.18)
    return jnp.clip(strengthened(values, jax.random.fold_in(key, 3), *heavy), -reach, reach).astype(held_as)


def setup_inputs(seed: int = 0) -> dict:
    keys = jax.random.split(jax.random.key(seed), 12)
    return {
        "inputs": gaussian_with(keys[0], (MB, SEQ, D), 1.0, 6.0, ((1, 16),), (1, 2, 16, 2.0)),
        "cotangent": noise(keys[1], (MB, SEQ, D), 1.0, 6.0, ((1, 16),)),
        "norm_attn": jnp.clip(1.0 + 0.18 * jax.random.normal(keys[2], (LAYERS, D), jnp.float32), 0.1, 1.9),
        "w_query": noise(keys[3], (LAYERS, D, H * HD), D ** -0.5, 0.15625, ((0, 2), (2, 2))),
        "w_key": noise(keys[4], (LAYERS, D, KV * HD), D ** -0.5, 0.15625, ((0, 2), (2, 2))),
        "w_value": noise(keys[5], (LAYERS, D, KV * HD), D ** -0.5, 0.15625, ((0, 2), (2, 2))),
        "w_out": noise(keys[6], (LAYERS, D, H * HD), (max(1, 5 * H * HD // SEQ)) ** -0.5, 2.0, ((0, 2), (2, 2))),
        "norm_mlp": jnp.clip(1.0 + 0.18 * jax.random.normal(keys[7], (LAYERS, D), jnp.float32), 0.1, 1.9),
        "w_gate": noise(keys[8], (LAYERS, D, FF), D ** -0.5, 0.15625, ((0, 2), (2, 2))),
        "w_up": noise(keys[9], (LAYERS, D, FF), D ** -0.5, 0.15625, ((0, 2), (2, 2))),
        "w_down": noise(keys[10], (LAYERS, D, FF), FF ** -0.5, 0.09375, ((0, 2), (2, 2))),
    }


@jax.custom_vjp
def low(v):
    return lax.optimization_barrier(v.astype(jnp.bfloat16)).astype(jnp.float32)

@jax.custom_vjp
def low_back(v):
    return v

def low_keep(v):
    return (low(v), None)

def low_pass(kept, grad):
    return (grad,)

def back_keep(v):
    return (v, None)

def back_low(kept, grad):
    return (low(grad),)
low.defvjp(low_keep, low_pass)
low_back.defvjp(back_keep, back_low)
highest = lax.Precision.HIGHEST
epsilon = 1e-05
base_theta = 100000.0

def mat_mul(left_op, right_op):
    return jnp.dot(left_op, right_op, precision=highest)

def mat_mul_t(left_op, right_op):
    return lax.dot_general(left_op, right_op, (((1,), (1,)), ((), ())), precision=highest)

def place_rows(row_ids, half_rows, halves):
    block_id = row_ids // half_rows
    pair_id = block_id // 2
    pos_block = jnp.where(block_id % 2 == 0, pair_id, halves - 1 - pair_id)
    return pos_block * half_rows + row_ids % half_rows

def rotary_tables(positions):
    frequency = base_theta ** (-jnp.arange(0, HD, 2).astype(jnp.float32) / HD)
    angles = positions.astype(jnp.float32)[:, None] * frequency[None, :]
    angles = jnp.concatenate([angles, angles], axis=1)
    return (jnp.cos(angles), jnp.sin(angles))

def rotate(values, cosine, sine_tab, sign_val):
    half_dim = values.shape[-1] // 2
    swapped = jnp.concatenate([-values[..., half_dim:], values[..., :half_dim]], axis=-1)
    return values * cosine[:, None, :] + sign_val * swapped * sine_tab[:, None, :]

def rms_norm(values, gain_vec):
    return values * lax.rsqrt(lax.optimization_barrier(jnp.mean(values * values, axis=-1, keepdims=True)) + epsilon) * gain_vec

def attend(queries, keys_all, values_all, positions):
    repeat = H // KV
    keys_wide = jnp.repeat(keys_all, repeat, axis=1)
    values_wide = jnp.repeat(values_all, repeat, axis=1)
    block_rows = math.gcd(SEQ, 512)

    def one_block(block_id):
        query_rows = lax.dynamic_slice_in_dim(queries, block_id * block_rows, block_rows, 0)
        query_pos = lax.dynamic_slice_in_dim(positions, block_id * block_rows, block_rows, 0)
        scores = low_back(jnp.einsum('qhd,khd->hqk', query_rows, keys_wide, precision=highest) * HD ** (-0.5))
        scores = jnp.where(query_pos[None, :, None] >= positions[None, None, :], scores, -jnp.inf)
        top_score = lax.optimization_barrier(jnp.max(scores, axis=-1, keepdims=True))
        exp_scores = jnp.exp(scores - top_score)
        weights_p = exp_scores / lax.optimization_barrier(jnp.sum(exp_scores, axis=-1, keepdims=True))
        return jnp.einsum('hqk,khd->qhd', low(weights_p), values_wide, precision=highest)
    blocks = lax.map(jax.checkpoint(one_block), jnp.arange(SEQ // block_rows, dtype=jnp.int32))
    return blocks.reshape(SEQ, H * HD)

def residual_block(hidden_in, params, cosine, sine_tab, positions):
    gain_attn, query_w, key_w, value_w, out_w, gain_mlp, gate_w, up_w, down_w = params
    normed = low(rms_norm(hidden_in, gain_attn))
    queries = low(rotate(low_back(mat_mul(normed, query_w)).reshape(SEQ, H, HD), cosine, sine_tab, 1.0))
    keys_all = low(rotate(low_back(mat_mul(normed, key_w)).reshape(SEQ, KV, HD), cosine, sine_tab, 1.0))
    values_all = low(low_back(mat_mul(normed, value_w))).reshape(SEQ, KV, HD)
    mixed_out = low(low_back(attend(queries, keys_all, values_all, positions)))
    middle = hidden_in + low_back(mat_mul_t(mixed_out, out_w))
    normed_mlp = low(rms_norm(middle, gain_mlp))
    gate_pre = low_back(mat_mul(normed_mlp, gate_w))
    up_pre = low_back(mat_mul(normed_mlp, up_w))
    inner_act = low(gate_pre * jax.nn.sigmoid(gate_pre) * up_pre)
    return middle + low_back(mat_mul_t(inner_act, down_w))

def reference(inputs, cotangent, norm_attn, w_query, w_key, w_value, w_out, norm_mlp, w_gate, w_up, w_down):
    positions = place_rows(jnp.arange(SEQ, dtype=jnp.int32), SPAN // 2, 2 * SEQ // SPAN)
    cosine, sine_tab = rotary_tables(positions)
    stacked = (norm_attn, w_query, w_key, w_value, w_out, norm_mlp, w_gate, w_up, w_down)
    current = inputs.astype(jnp.float32)
    section_vals = []
    pullers = []
    for section_id in range(LAYERS):
        params = tuple((weight[section_id].astype(jnp.float32) for weight in stacked))
        is_last = section_id == LAYERS - 1

        def run_section(section_in, section_params, is_last=is_last):
            result = lax.map(lambda one_seq: residual_block(one_seq, section_params, cosine, sine_tab, positions), section_in)
            return low(result) if is_last else low_back(low(result))
        value_out, pull_back = jax.vjp(run_section, current, params)
        section_vals.append(value_out)
        pullers.append(pull_back)
        current = value_out
    grad_in = cotangent.astype(jnp.float32)
    input_list = [None] * LAYERS
    weight_list = [None] * LAYERS
    for section_id in reversed(range(LAYERS)):
        grad_in, weight_grads = pullers[section_id](grad_in)
        input_list[section_id] = grad_in
        weight_list[section_id] = weight_grads
    grouped = [jnp.stack([weight_list[section_id][index_at] for section_id in range(LAYERS)]) for index_at in range(9)]
    return (jnp.stack(section_vals).astype(jnp.bfloat16), jnp.stack(input_list), grouped[0], grouped[1], grouped[2], grouped[3], grouped[4], grouped[5], grouped[6], grouped[7], grouped[8])
```

```python
import jax
import jax.numpy as jnp
from jax import lax
from jax.experimental import pallas as pl
from jax.experimental.pallas import tpu as pltpu
from jax.sharding import PartitionSpec as P

HD = 96


epsilon = 1e-05
base_theta = 100000.0


def shifted(array, axis, by):
    size = lax.axis_size(axis)
    pairs = [(i, i + by) for i in range(size) if 0 <= i + by < size]
    return lax.ppermute(array, axis, pairs)


def place_rows(row_ids, half_rows, halves):
    block_id = row_ids // half_rows
    pair_id = block_id // 2
    pos_block = jnp.where(block_id % 2 == 0, pair_id, halves - 1 - pair_id)
    return pos_block * half_rows + row_ids % half_rows


def rotary_tables(positions):
    frequency = base_theta ** (-jnp.arange(0, HD, 2).astype(jnp.float32) / HD)
    angles = positions.astype(jnp.float32)[:, None] * frequency[None, :]
    angles = jnp.concatenate([angles, angles], axis=1)
    return (jnp.cos(angles), jnp.sin(angles))


def rotate(values, cosine, sine_tab, sign_val):
    half_dim = values.shape[-1] // 2
    swapped = jnp.concatenate([-values[..., half_dim:], values[..., :half_dim]], axis=-1)
    return values * cosine[:, None, :] + sign_val * swapped * sine_tab[:, None, :]


def normalize(values, gain_vec):
    inv_scale = lax.rsqrt(jnp.mean(values * values, axis=-1, keepdims=True) + epsilon)
    normed = values * inv_scale
    return (normed * gain_vec, normed, inv_scale)


def norm_back(upstream, normed, inv_scale, gain_vec):
    scaled = upstream * gain_vec
    down_grad = inv_scale * (scaled - normed * jnp.mean(scaled * normed, axis=-1, keepdims=True))
    return (down_grad, jnp.sum(upstream * normed, axis=0))


def dot_plain(left_op, right_op):
    return jnp.dot(left_op, right_op, preferred_element_type=jnp.float32)


def dot_right_t(left_op, right_op):
    return lax.dot_general(
        left_op, right_op, (((1,), (1,)), ((), ())), preferred_element_type=jnp.float32
    )


def dot_left_t(left_op, right_op):
    return lax.dot_general(
        left_op, right_op, (((0,), (0,)), ((), ())), preferred_element_type=jnp.float32
    )


def score_block(queries, keys_part, query_pos, key_pos, groups):
    query_count = queries.shape[0]
    key_count = keys_part.shape[0]
    query4 = queries.reshape(query_count, groups, -1, HD)
    key_rows3 = keys_part.reshape(key_count, groups, HD)
    scores = jnp.einsum(
        "qgrd,kgd->grqk", query4, key_rows3, preferred_element_type=jnp.float32
    ) * HD ** (-0.5)
    return (scores, query_pos[:, None] >= key_pos[None, :])


def reduce_grads(grad_set):
    return (
        lax.psum_scatter(
            grad_set[0].astype(jnp.bfloat16), "ctx", scatter_dimension=0, tiled=True
        ).astype(jnp.float32),
        lax.psum_scatter(
            grad_set[1].astype(jnp.bfloat16), "ctx", scatter_dimension=0, tiled=True
        ).astype(jnp.float32),
        lax.psum_scatter(
            grad_set[2].astype(jnp.bfloat16), "ctx", scatter_dimension=0, tiled=True
        ).astype(jnp.float32),
        lax.psum_scatter(
            grad_set[3].astype(jnp.bfloat16), "ctx", scatter_dimension=0, tiled=True
        ).astype(jnp.float32),
        lax.psum_scatter(
            grad_set[4].astype(jnp.bfloat16), "ctx", scatter_dimension=0, tiled=True
        ).astype(jnp.float32),
        lax.psum_scatter(
            grad_set[5].astype(jnp.bfloat16), "ctx", scatter_dimension=0, tiled=True
        ).astype(jnp.float32),
        lax.psum_scatter(
            grad_set[6].astype(jnp.bfloat16), "ctx", scatter_dimension=0, tiled=True
        ).astype(jnp.float32),
        lax.psum_scatter(
            grad_set[7].astype(jnp.bfloat16), "ctx", scatter_dimension=0, tiled=True
        ).astype(jnp.float32),
        lax.psum_scatter(
            grad_set[8].astype(jnp.bfloat16), "ctx", scatter_dimension=0, tiled=True
        ).astype(jnp.float32),
    )


def on_device_wide(
    inputs, cotangent, norm_attn, w_query, w_key, w_value, w_out, norm_mlp, w_gate, w_up, w_down
):
    params = (
        norm_attn[0],
        w_query[0],
        w_key[0],
        w_value[0],
        w_out[0],
        norm_mlp[0],
        w_gate[0],
        w_up[0],
        w_down[0],
    )
    gain_attn, query_w, key_w, value_w, out_w, gain_mlp, gate_w, up_w, down_w = params
    batches, local_rows, model_width = inputs.shape
    span_rows = local_rows * lax.axis_size("tp")
    seq_len = span_rows * lax.axis_size("ctx")
    half_rows = span_rows // 2
    halves = 2 * lax.axis_size("ctx")
    groups = key_w.shape[1] // HD
    head_count = query_w.shape[1] // HD
    repeat = head_count // groups
    kv_width = groups * HD
    section_at = lax.axis_index("pipe")
    sections = lax.axis_size("pipe")
    ctx_at = lax.axis_index("ctx")
    own_pos = place_rows(
        ctx_at * span_rows + jnp.arange(span_rows, dtype=jnp.int32), half_rows, halves
    )
    all_pos = place_rows(jnp.arange(seq_len, dtype=jnp.int32), half_rows, halves)
    cosine, sine_tab = rotary_tables(own_pos)
    kept_bufs = None
    section_out = jnp.zeros((batches, local_rows, model_width), jnp.bfloat16)
    outgoing = jnp.zeros((local_rows, model_width), jnp.bfloat16)
    for tick_at in range(batches + sections - 1):
        arrived = shifted(outgoing, "pipe", 1)
        slot_raw = tick_at - section_at
        is_live = (slot_raw >= 0) & (slot_raw < batches)
        slot_at = jnp.clip(slot_raw, 0, batches - 1)
        section_in = jnp.where(section_at == 0, inputs[min(tick_at, batches - 1)], arrived).astype(
            jnp.float32
        )
        normed_attn = normalize(section_in, gain_attn)[0]
        forward_attn_full = lax.all_gather(
            normed_attn.astype(jnp.bfloat16), "tp", axis=0, tiled=True
        )
        forward_queries = rotate(
            dot_plain(forward_attn_full, query_w).reshape(span_rows, head_count, HD),
            cosine,
            sine_tab,
            1.0,
        )
        forward_queries = forward_queries.reshape(span_rows, head_count * HD).astype(jnp.bfloat16)
        keys_own = rotate(
            dot_plain(forward_attn_full, key_w).reshape(span_rows, groups, HD),
            cosine,
            sine_tab,
            1.0,
        )
        keys_own = keys_own.reshape(span_rows, kv_width).astype(jnp.bfloat16)
        values_own = dot_plain(forward_attn_full, value_w).astype(jnp.bfloat16)
        forward_keys_all = lax.all_gather(keys_own, "ctx", axis=0, tiled=True)
        forward_values_all = lax.all_gather(values_own, "ctx", axis=0, tiled=True)
        forward_scores, forward_allowed = score_block(
            forward_queries, forward_keys_all, own_pos, all_pos, groups
        )
        forward_scores = jnp.where(forward_allowed, forward_scores, -jnp.inf)
        top_score = jnp.max(forward_scores, axis=-1, keepdims=True)
        exp_scores = jnp.exp(forward_scores - top_score)
        totals = jnp.sum(exp_scores, axis=-1, keepdims=True)
        forward_prob_low = (exp_scores / totals).astype(jnp.bfloat16)
        mixed4 = jnp.einsum(
            "grqk,kgd->qgrd",
            forward_prob_low,
            forward_values_all.reshape(seq_len, groups, HD),
            preferred_element_type=jnp.float32,
        )
        forward_mixed_out = mixed4.reshape(span_rows, head_count * HD).astype(jnp.bfloat16)
        forward_log_total = top_score[..., 0] + jnp.log(totals[..., 0])
        forward_middle = section_in + lax.psum_scatter(
            dot_right_t(forward_mixed_out, out_w).astype(jnp.bfloat16),
            "tp",
            scatter_dimension=0,
            tiled=True,
        ).astype(jnp.float32)
        normed_mlp = normalize(forward_middle, gain_mlp)[0]
        forward_mlp_full = lax.all_gather(normed_mlp.astype(jnp.bfloat16), "tp", axis=0, tiled=True)
        forward_gate_pre = dot_plain(forward_mlp_full, gate_w)
        forward_up_pre = dot_plain(forward_mlp_full, up_w)
        forward_inner_act = (
            forward_gate_pre * jax.nn.sigmoid(forward_gate_pre) * forward_up_pre
        ).astype(jnp.bfloat16)
        result = forward_middle + lax.psum_scatter(
            dot_right_t(forward_inner_act, down_w).astype(jnp.bfloat16),
            "tp",
            scatter_dimension=0,
            tiled=True,
        ).astype(jnp.float32)
        forward_kept_acts = (
            section_in,
            forward_attn_full,
            forward_queries,
            forward_keys_all,
            forward_values_all,
            forward_mixed_out,
            forward_log_total,
            forward_middle,
            forward_mlp_full,
            forward_gate_pre,
            forward_up_pre,
        )
        result, kept_acts = (result, forward_kept_acts)
        if kept_bufs is None:
            kept_bufs = tuple(
                (
                    jnp.zeros((batches,) + piece_act.shape, piece_act.dtype)
                    for piece_act in kept_acts
                )
            )
        kept_bufs = tuple(
            (
                jnp.where(is_live, buffer.at[slot_at].set(piece_act), buffer)
                for buffer, piece_act in zip(kept_bufs, kept_acts)
            )
        )
        outgoing = result.astype(jnp.bfloat16)
        section_out = jnp.where(is_live, section_out.at[slot_at].set(outgoing), section_out)
    input_grads = jnp.zeros((batches, local_rows, model_width), jnp.float32)
    grad_acc = tuple((jnp.zeros(weight.shape, jnp.float32) for weight in params))
    outgoing = jnp.zeros((local_rows, model_width), jnp.bfloat16)
    for tick_at in range(batches + sections - 1):
        arrived = shifted(outgoing, "pipe", -1)
        slot_raw = tick_at - (sections - 1 - section_at)
        is_live = (slot_raw >= 0) & (slot_raw < batches)
        slot_at = jnp.clip(slot_raw, 0, batches - 1)
        upstream = jnp.where(
            section_at == sections - 1,
            cotangent[slot_at].astype(jnp.float32),
            arrived.astype(jnp.float32),
        )
        (
            hidden_in,
            attn_full,
            queries,
            keys_all,
            values_all,
            mixed_out,
            log_total,
            middle,
            mlp_full,
            gate_pre,
            up_pre,
        ) = tuple((buffer[slot_at] for buffer in kept_bufs))
        branch_full = lax.all_gather(upstream.astype(jnp.bfloat16), "tp", axis=0, tiled=True)
        sigmoid_g = jax.nn.sigmoid(gate_pre)
        silu_gate = gate_pre * sigmoid_g
        inner_act = (silu_gate * up_pre).astype(jnp.bfloat16)
        grad_down = dot_left_t(branch_full, inner_act)
        inner_grad = dot_plain(branch_full, down_w)
        gate_grad = (inner_grad * up_pre * sigmoid_g * (1.0 + gate_pre * (1.0 - sigmoid_g))).astype(
            jnp.bfloat16
        )
        up_grad = (inner_grad * silu_gate).astype(jnp.bfloat16)
        grad_gate = dot_left_t(mlp_full, gate_grad)
        grad_up = dot_left_t(mlp_full, up_grad)
        normed_grad = lax.psum_scatter(
            (dot_right_t(gate_grad, gate_w) + dot_right_t(up_grad, up_w)).astype(jnp.bfloat16),
            "tp",
            scatter_dimension=0,
            tiled=True,
        ).astype(jnp.float32)
        second_norm = normalize(middle, gain_mlp)
        middle_norm_grad, grad_gain_mlp = norm_back(
            normed_grad, second_norm[1], second_norm[2], gain_mlp
        )
        middle_grad = upstream + middle_norm_grad
        attn_out_full = lax.all_gather(middle_grad.astype(jnp.bfloat16), "tp", axis=0, tiled=True)
        grad_out = dot_left_t(attn_out_full, mixed_out)
        mixed_grad = dot_plain(attn_out_full, out_w).astype(jnp.bfloat16)
        scores, allowed = score_block(queries, keys_all, own_pos, all_pos, groups)
        prob_f32 = jnp.where(allowed, jnp.exp(scores - log_total[..., None]), 0.0)
        grad_rows4 = mixed_grad.reshape(span_rows, groups, repeat, HD)
        prob_grad = jnp.einsum(
            "qgrd,kgd->grqk",
            grad_rows4,
            values_all.reshape(seq_len, groups, HD),
            preferred_element_type=jnp.float32,
        )
        inner_sum = jnp.sum(prob_f32 * prob_grad, axis=-1, keepdims=True)
        score_grad = (prob_f32 * (prob_grad - inner_sum)).astype(jnp.bfloat16)
        prob_low = prob_f32.astype(jnp.bfloat16)
        query_grad4 = jnp.einsum(
            "grqk,kgd->qgrd",
            score_grad,
            keys_all.reshape(seq_len, groups, HD),
            preferred_element_type=jnp.float32,
        ) * HD ** (-0.5)
        query4 = queries.reshape(span_rows, groups, repeat, HD)
        key_part = jnp.einsum(
            "grqk,qgrd->kgd", score_grad, query4, preferred_element_type=jnp.float32
        ) * HD ** (-0.5)
        value_part = jnp.einsum(
            "grqk,qgrd->kgd", prob_low, grad_rows4, preferred_element_type=jnp.float32
        )
        key_value_grad = lax.psum_scatter(
            jnp.concatenate(
                [
                    key_part.reshape(span_rows * lax.axis_size("ctx"), kv_width),
                    value_part.reshape(span_rows * lax.axis_size("ctx"), kv_width),
                ],
                axis=1,
            ).astype(jnp.bfloat16),
            "ctx",
            scatter_dimension=0,
            tiled=True,
        ).astype(jnp.float32)
        key_sum = key_value_grad[:, :kv_width]
        value_sum = key_value_grad[:, kv_width:]
        query_grad = rotate(query_grad4.reshape(span_rows, head_count, HD), cosine, sine_tab, -1.0)
        query_grad = query_grad.reshape(span_rows, head_count * HD).astype(jnp.bfloat16)
        key_grad = rotate(key_sum.reshape(span_rows, groups, HD), cosine, sine_tab, -1.0)
        key_grad = key_grad.reshape(span_rows, kv_width).astype(jnp.bfloat16)
        value_grad = value_sum.astype(jnp.bfloat16)
        grad_query = dot_left_t(attn_full, query_grad)
        grad_key = dot_left_t(attn_full, key_grad)
        grad_value = dot_left_t(attn_full, value_grad)
        total_q = dot_right_t(query_grad, query_w)
        total_k = dot_right_t(key_grad, key_w)
        attn_grad = lax.psum_scatter(
            (total_q + total_k + dot_right_t(value_grad, value_w)).astype(jnp.bfloat16),
            "tp",
            scatter_dimension=0,
            tiled=True,
        ).astype(jnp.float32)
        first_norm = normalize(hidden_in, gain_attn)
        input_norm_grad, grad_gain_attn = norm_back(
            attn_grad, first_norm[1], first_norm[2], gain_attn
        )
        grad_set = (
            grad_gain_attn,
            grad_query,
            grad_key,
            grad_value,
            grad_out,
            grad_gain_mlp,
            grad_gate,
            grad_up,
            grad_down,
        )
        down_grad, grad_set = (middle_grad + input_norm_grad, grad_set)
        outgoing = down_grad.astype(jnp.bfloat16)
        input_grads = jnp.where(is_live, input_grads.at[slot_at].set(down_grad), input_grads)
        masked = tuple((jnp.where(is_live, grad_one, 0.0) for grad_one in grad_set))
        grad_acc = tuple((acc_one + new_one for acc_one, new_one in zip(grad_acc, masked)))
    summed = reduce_grads(grad_acc)
    gain_one, gain_two = lax.psum((summed[0], summed[5]), "tp")
    return (
        section_out[None],
        input_grads[None],
        gain_one[None],
        summed[1][None],
        summed[2][None],
        summed[3][None],
        summed[4][None],
        gain_two[None],
        summed[6][None],
        summed[7][None],
        summed[8][None],
    )


MIB = 1 << 20
CORE, SEQ, CTX, SECTION = range(4)
LOG2E = 1.4426950408889634


def in_hbm(array):
    return pltpu.with_memory_space_constraint(array, pltpu.HBM)


def in_vmem(array):
    return pltpu.with_memory_space_constraint(array, pltpu.VMEM)


HBM = pl.BlockSpec(memory_space=pltpu.HBM)
VMEM = pl.BlockSpec(memory_space=pltpu.VMEM)
SCALARS = pl.BlockSpec(memory_space=pltpu.SMEM)


def whole_call(
    body, outs, scratch=(), flops=0, nbytes=0, grant=16, in_specs=None, out_specs=None
):
    specs = {} if in_specs is None else {"in_specs": in_specs}
    specs |= {} if out_specs is None else {"out_specs": out_specs}
    return pl.pallas_call(
        body,
        out_shape=outs,
        scratch_shapes=scratch,
        compiler_params=pltpu.CompilerParams(vmem_limit_bytes=grant * MIB),
        cost_estimate=pl.CostEstimate(flops=flops, bytes_accessed=nbytes, transcendentals=0),
        **specs,
    )


def load_weights(weights):
    count = len(weights)

    def body(*refs):
        copies = [
            pltpu.make_async_copy(refs[at], refs[count + at], refs[-1].at[at])
            for at in range(count)
        ]
        for copy in copies:
            copy.start()
        for copy in copies:
            copy.wait()

    return whole_call(
        body,
        tuple(pltpu.VMEM(weight.shape, weight.dtype) for weight in weights),
        scratch=[pltpu.SemaphoreType.DMA((count,))],
        nbytes=2 * sum(weight.size for weight in weights),
        grant=4,
        in_specs=[HBM] * count,
        out_specs=(VMEM,) * count,
    )(*map(in_hbm, weights))


def own_half(rows, core, batches):
    parts = rows.reshape(batches, 2, rows.shape[0] // batches // 2, rows.shape[1])
    return jnp.where(core == 0, parts[:, 0], parts[:, 1])


class Outbox:
    def __init__(self, sems):
        self.sems, self.copies = sems, []

    def send(self, staged, target):
        copy = pltpu.make_async_copy(staged, target, self.sems.at[len(self.copies)])
        copy.start()
        self.copies.append(copy)

    def finish(self):
        for copy in self.copies:
            copy.wait()


def rotate_head(head, cosine, sine_tab):
    lower, upper = head[: HD // 2], head[HD // 2 :]
    return jnp.concatenate(
        [lower * cosine - upper * sine_tab, upper * cosine + lower * sine_tab], axis=0
    )


def rotate_back_head(head, cosine, sine_tab):
    return rotate_head(head, cosine, -sine_tab)


def project_heads(section_in, gain_vec, weights, cosine, sine_tab, indices):
    rows, width = section_in.shape
    batches = 2
    span = rows // batches
    groups = weights[1].shape[1] // HD
    repeat = weights[0].shape[1] // HD // groups

    def body(
        at_ref, in_ref, gain_ref, query_ref, key_ref, value_ref, cos_ref, sin_ref,
        mine_ref, theirs_ref, out_ref,
    ):
        cosine, sine_tab = cos_ref[...], sin_ref[...]
        normed = normalize(in_ref[...].astype(jnp.float32), gain_ref[...])[0].astype(jnp.bfloat16)
        mine_ref[...] = jnp.where(at_ref[SEQ] == 0, normed[:span], normed[span:])
        theirs_ref[...] = jnp.where(at_ref[SEQ] == 0, normed[span:], normed[:span])
        queries = dot_plain(normed, query_ref[...]).T
        keys = dot_plain(normed, key_ref[...]).T
        values = dot_plain(normed, value_ref[...]).T
        for group in range(groups):
            parts = [
                rotate_head(queries[head * HD : (head + 1) * HD], cosine, sine_tab)
                for head in range(group * repeat, (group + 1) * repeat)
            ]
            place = slice(group * HD, (group + 1) * HD)
            parts += [rotate_head(keys[place], cosine, sine_tab), values[place]]
            for at, part in enumerate(parts):
                part = part.astype(jnp.bfloat16)
                for seq in range(batches):
                    lanes = slice(seq * span, (seq + 1) * span)
                    out_ref[group * batches + seq, at * HD : (at + 1) * HD] = part[:, lanes]

    columns = sum(weight.shape[1] for weight in weights)
    return whole_call(
        body,
        (
            pltpu.HBM((span, width), jnp.bfloat16),
            pltpu.HBM((span, width), jnp.bfloat16),
            pltpu.HBM((groups * batches, (repeat + 2) * HD, span), jnp.bfloat16),
        ),
        flops=2 * rows * width * columns,
        nbytes=2 * width * columns,
        in_specs=[SCALARS] + [VMEM] * 7,
    )(indices, in_hbm(section_in), in_hbm(gain_vec[None]), *weights, cosine, sine_tab)


def side_by_side(ref, first, last, blocks=None):
    blocks = range(ref.shape[0]) if blocks is None else blocks
    return jnp.concatenate([ref[block, first:last] for block in blocks], axis=1)


def by_position(ref, first, last):
    blocks, _, span = ref.shape
    half = span // 2
    lower = [ref[block, first:last, :half] for block in range(blocks)]
    upper = [ref[block, first:last, half:] for block in reversed(range(blocks))]
    return jnp.concatenate(lower + upper, axis=1)


def to_blocks(ref, entries, rows, at):
    blocks, _, span = ref.shape
    half = span // 2
    for first in range(0, rows.shape[1], half):
        place = (at + first) // half
        part = rows[:, first : first + half]
        if place < blocks:
            ref[place, entries, :half] = part
        else:
            ref[2 * blocks - 1 - place, entries, half:] = part


TILE = 256


def masked(scores, outside):
    rows = scores.shape[0] - TILE
    key_at = lax.broadcasted_iota(jnp.int32, (TILE, TILE), 0)
    query_at = lax.broadcasted_iota(jnp.int32, (TILE, TILE), 1)
    last = jnp.where(key_at <= query_at, scores[rows:], outside)
    return last if rows == 0 else jnp.concatenate([scores[:rows], last], axis=0)


def attend_heads(head_qkv, repeat):
    blocks, _, span = head_qkv.shape
    seq_len = blocks * span
    scale = HD ** (-0.5) * LOG2E

    def body(in_ref, out_ref, log_ref):
        keys = by_position(in_ref, repeat * HD, (repeat + 1) * HD).T
        values = by_position(in_ref, (repeat + 1) * HD, (repeat + 2) * HD)
        for head in range(repeat):
            entries = slice(head * HD, (head + 1) * HD)
            queries = by_position(in_ref, entries.start, entries.stop)
            for first in range(0, seq_len, TILE):
                stop = first + TILE
                scores = masked(dot_plain(keys[:stop], queries[:, first:stop]), -jnp.inf)
                top_score = jnp.max(scores, axis=0, keepdims=True)
                exp_scores = jnp.exp2((scores - top_score) * scale)
                totals = jnp.sum(exp_scores, axis=0, keepdims=True)
                prob_low = (exp_scores * (1.0 / totals)).astype(jnp.bfloat16)
                mixed = dot_plain(values[:, :stop], prob_low).astype(jnp.bfloat16)
                to_blocks(out_ref, entries, mixed, first)
                log_ref[head, :, first:stop] = top_score * scale + jnp.log2(totals)

    return whole_call(
        body,
        (
            pltpu.HBM((blocks, repeat * HD, span), jnp.bfloat16),
            pltpu.HBM((repeat, 1, seq_len), jnp.float32),
        ),
        flops=4 * repeat * seq_len * seq_len * HD,
        nbytes=12 * seq_len * HD * repeat,
    )(in_hbm(head_qkv))


def attend_heads_back(head_qkv, head_grad, log_total, cosine, sine_tab, repeat):
    blocks, _, span = head_qkv.shape
    seq_len = blocks * span
    scale = HD ** (-0.5)
    key_place = slice(repeat * HD, (repeat + 1) * HD)
    value_place = slice((repeat + 1) * HD, (repeat + 2) * HD)

    def body(in_ref, grad_ref, log_ref, cos_ref, sin_ref, out_ref, key_acc, value_acc):
        keys_t = by_position(in_ref, key_place.start, key_place.stop)
        keys = keys_t.T
        values = by_position(in_ref, value_place.start, value_place.stop).T
        key_acc[...] = jnp.zeros_like(key_acc)
        value_acc[...] = jnp.zeros_like(value_acc)
        for head in range(repeat):
            entries = slice(head * HD, (head + 1) * HD)
            all_queries = by_position(in_ref, entries.start, entries.stop)
            all_grads = by_position(grad_ref, entries.start, entries.stop)
            for first in range(0, seq_len, TILE):
                stop = first + TILE
                place = slice(first, stop)
                queries, grads = all_queries[:, place], all_grads[:, place]
                scores = dot_plain(keys[:stop], queries) * (scale * LOG2E)
                prob = jnp.exp2(masked(scores - log_ref[head, :, place], -jnp.inf))
                prob_grad = dot_plain(values[:stop], grads)
                inner_sum = jnp.sum(prob * prob_grad, axis=0, keepdims=True)
                score_grad = (prob * (prob_grad - inner_sum)).astype(jnp.bfloat16)
                prob_low = prob.astype(jnp.bfloat16)
                query_grad = rotate_back_head(
                    dot_plain(keys_t[:, :stop], score_grad) * scale,
                    cos_ref[:, place],
                    sin_ref[:, place],
                ).astype(jnp.bfloat16)
                to_blocks(out_ref, entries, query_grad, first)
                key_acc[:, :stop] += dot_right_t(queries, score_grad)
                value_acc[:, :stop] += dot_right_t(grads, prob_low)
        key_grad = rotate_back_head(key_acc[...] * scale, cos_ref[...], sin_ref[...])
        to_blocks(out_ref, key_place, key_grad.astype(jnp.bfloat16), 0)
        to_blocks(out_ref, value_place, value_acc[...].astype(jnp.bfloat16), 0)

    return whole_call(
        body,
        pltpu.HBM(head_qkv.shape, jnp.bfloat16),
        scratch=[pltpu.VMEM((HD, seq_len), jnp.float32)] * 2,
        flops=10 * repeat * seq_len * seq_len * HD,
        nbytes=16 * repeat * seq_len * HD,
    )(in_hbm(head_qkv), head_grad, *map(in_hbm, (log_total, cosine, sine_tab)))


def rows_side_by_side(ref, first, last, batches):
    groups = ref.shape[0] // batches
    return jnp.concatenate(
        [
            side_by_side(
                ref, first, last, [group * batches + seq for seq in range(batches)]
            )
            for group in range(groups)
        ],
        axis=0,
    )


def project_out(arrived, out_w, batches):
    _, depth, span = arrived.shape
    width, heads = out_w.shape
    rows = batches * span

    def body(in_ref, weight_ref, mixed_ref, out_ref):
        mixed = rows_side_by_side(in_ref, 0, depth, batches)
        mixed_ref[...] = mixed.T
        out_ref[...] = dot_plain(weight_ref[...], mixed).T.astype(jnp.bfloat16)

    return whole_call(
        body,
        (
            pltpu.HBM((rows, heads), jnp.bfloat16),
            pltpu.HBM((rows, width), jnp.bfloat16),
        ),
        flops=2 * rows * width * heads,
        nbytes=2 * width * heads,
    )(arrived, out_w)


def full_block(array):
    return pl.BlockSpec(
        array.shape, lambda *_: (0,) * len(array.shape), pipeline_mode=pl.Buffered(1)
    )


def stepped_call(
    body, indices, grid, in_specs, outs, out_specs, scratch, flops, nbytes, grant, aliases=None
):
    call = pl.pallas_call(
        body,
        grid_spec=pltpu.PrefetchScalarGridSpec(
            num_scalar_prefetch=1,
            grid=grid,
            in_specs=in_specs,
            out_specs=out_specs,
            scratch_shapes=scratch,
        ),
        out_shape=outs,
        input_output_aliases=aliases or {},
        compiler_params=pltpu.CompilerParams(
            dimension_semantics=("arbitrary",) * len(grid), vmem_limit_bytes=grant * MIB
        ),
        cost_estimate=pl.CostEstimate(flops=flops, bytes_accessed=nbytes, transcendentals=0),
    )
    return lambda *arrays: call(indices, *arrays)


def weight_slots(count, width):
    return [
        pltpu.VMEM((2, count, width, HIDDEN), jnp.bfloat16),
        pltpu.SemaphoreType.DMA((2, count)),
    ]


class Stream:
    def __init__(self, weights, slots, sems, steps, first=0):
        self.weights, self.slots, self.sems, self.first = weights, slots, sems, first
        self.step, self.begins = pl.program_id(0), pl.program_id(1) == 0

        @pl.when(self.begins & (self.step == 0))
        def _():
            for copy in self.copies(0):
                copy.start()

        @pl.when(self.begins & (self.step + 1 < steps))
        def _():
            for copy in self.copies(self.step + 1):
                copy.start()

    def copies(self, step):
        slot = step % 2
        first = pl.multiple_of((self.first + step) * HIDDEN, HIDDEN)
        place = pl.ds(first, HIDDEN)
        return [
            pltpu.make_async_copy(
                weight.at[:, place], self.slots.at[slot, at], self.sems.at[slot, at]
            )
            for at, weight in enumerate(self.weights)
        ]

    def blocks(self):
        @pl.when(self.begins)
        def _():
            for copy in self.copies(self.step):
                copy.wait()

        return [self.slots[self.step % 2, at] for at in range(len(self.weights))]


def hidden_factors(gate_pre, up_pre):
    sigmoid_g = 0.5 + 0.5 * jnp.tanh(0.5 * gate_pre)
    silu_gate = gate_pre * sigmoid_g
    return silu_gate * up_pre, up_pre * (sigmoid_g + silu_gate * (1.0 - sigmoid_g)), silu_gate


HIDDEN = 512


class Blocks:
    def __init__(self, weights, held, sems):
        self.held = held
        hidden = weights[0].shape[1]
        self.places = [slice(first, first + HIDDEN) for first in range(0, hidden, HIDDEN)]
        self.copies = [
            [
                pltpu.make_async_copy(
                    weight.at[:, place], held.at[at, step], sems.at[at, step]
                )
                for at, weight in enumerate(weights)
            ]
            for step, place in enumerate(self.places)
        ]
        self.start(0)

    def start(self, step):
        for copy in self.copies[step]:
            copy.start()

    def get(self, step, at):
        self.copies[step][at].wait()
        return self.held[at, step]


def block_scratch(weights):
    width, hidden = weights[0].shape
    count, steps = len(weights), hidden // HIDDEN
    return [
        pltpu.VMEM((count, steps, width, HIDDEN), jnp.bfloat16),
        pltpu.SemaphoreType.DMA((count, steps)),
    ]


def feed_forward(section_in, attn_own, attn_other, gain_vec, weights, batches, indices):
    rows, width = section_in.shape
    hidden = weights[0].shape[1]
    half = (batches, rows // batches // 2, width)

    def body(
        at_ref, in_ref, own_ref, other_ref, gain_ref, gate_ref, up_ref, down_ref,
        mid_out, low_out, gate_f_out, up_f_out, keep_out, send_out,
        mid_ref, low_ref, gate_f_ref, up_f_ref, keep_ref, send_ref, sems, held, block_sems,
    ):
        blocks = Blocks((gate_ref, up_ref, down_ref), held, block_sems)
        for step in range(1, len(blocks.places)):
            blocks.start(step)
        outbox = Outbox(sems)
        middle = in_ref[...].astype(jnp.float32) + (
            own_ref[...].astype(jnp.float32) + other_ref[...].astype(jnp.float32)
        )
        mid_ref[...] = middle
        outbox.send(mid_ref, mid_out)
        low = normalize(middle, gain_ref[...])[0].astype(jnp.bfloat16)
        low_ref[...] = own_half(low, at_ref[CORE], batches)
        outbox.send(low_ref, low_out)
        total = None
        for step, place in enumerate(blocks.places):
            inner, gate_f, up_f = hidden_factors(
                dot_plain(low, blocks.get(step, 0)), dot_plain(low, blocks.get(step, 1))
            )
            gate_f_ref[:, place] = gate_f.astype(jnp.bfloat16)
            up_f_ref[:, place] = up_f.astype(jnp.bfloat16)
            part = dot_right_t(inner.astype(jnp.bfloat16), blocks.get(step, 2))
            total = part if total is None else total + part
        outbox.send(gate_f_ref, gate_f_out)
        outbox.send(up_f_ref, up_f_out)
        total = total.astype(jnp.bfloat16)
        keep_ref[...] = own_half(total, at_ref[CORE], batches)
        send_ref[...] = own_half(total, 1 - at_ref[CORE], batches)
        outbox.send(send_ref, send_out)
        outbox.send(keep_ref, keep_out)
        outbox.finish()

    shapes = [
        ((rows, width), jnp.float32),
        (half, jnp.bfloat16),
        ((rows, hidden), jnp.bfloat16),
        ((rows, hidden), jnp.bfloat16),
        (half, jnp.bfloat16),
        (half, jnp.bfloat16),
    ]
    return whole_call(
        body,
        tuple(pltpu.HBM(*shape) for shape in shapes),
        scratch=[pltpu.VMEM(*shape) for shape in shapes]
        + [pltpu.SemaphoreType.DMA((len(shapes),))]
        + block_scratch(weights),
        flops=6 * rows * width * hidden,
        nbytes=6 * width * hidden,
        grant=36,
        in_specs=[SCALARS] + [VMEM] * 4 + [HBM] * 3,
        out_specs=(HBM,) * len(shapes),
    )(
        indices, in_hbm(section_in), in_hbm(attn_own), attn_other, in_hbm(gain_vec[None]),
        *map(in_hbm, weights),
    )


def feed_forward_back(upstream, gate_f, up_f, weights):
    rows, width = upstream.shape
    hidden = weights[0].shape[1]

    def body(
        upstream_ref, gate_f_ref, up_f_ref, down_ref, gate_ref, up_ref, out_ref, held, block_sems
    ):
        blocks = Blocks((down_ref, gate_ref, up_ref), held, block_sems)
        for step in range(1, len(blocks.places)):
            blocks.start(step)
        low = upstream_ref[...]
        total = None
        for step, place in enumerate(blocks.places):
            inner_grad = dot_plain(low, blocks.get(step, 0))
            gate_grad = (inner_grad * gate_f_ref[:, place].astype(jnp.float32)).astype(jnp.bfloat16)
            up_grad = (inner_grad * up_f_ref[:, place].astype(jnp.float32)).astype(jnp.bfloat16)
            part = dot_right_t(gate_grad, blocks.get(step, 1))
            part += dot_right_t(up_grad, blocks.get(step, 2))
            total = part if total is None else total + part
        out_ref[...] = total.astype(jnp.bfloat16)

    return whole_call(
        body,
        pltpu.HBM((rows, width), jnp.bfloat16),
        scratch=block_scratch(weights),
        flops=6 * rows * width * hidden,
        nbytes=6 * width * hidden,
        grant=34,
        in_specs=[VMEM] * 3 + [HBM] * 3,
    )(*map(in_hbm, (upstream, gate_f, up_f, weights[2], *weights[:2])))


def middle_back(
    upstream, part_own, part_other, middle, gain_vec, out_w, groups, batches, indices
):
    rows, width = middle.shape
    span = rows // batches
    depth = out_w.shape[1] // groups

    def body(
        at_ref, up_ref, own_ref, other_ref, mid_ref, gain_ref, weight_ref, grad_out, low_out, head_out,
        grad_ref, low_ref, head_ref, sems,
    ):
        outbox = Outbox(sems)
        normed_grad = own_ref[...].astype(jnp.float32) + other_ref[...].astype(jnp.float32)
        _, normed, inv_scale = normalize(mid_ref[...], gain_ref[...])
        down_grad = norm_back(normed_grad, normed, inv_scale, gain_ref[...])[0]
        middle_grad = up_ref[...].astype(jnp.float32) + down_grad
        grad_ref[...] = own_half(middle_grad, at_ref[CORE], batches)
        outbox.send(grad_ref, grad_out)
        low = middle_grad.astype(jnp.bfloat16)
        low_ref[...] = low
        outbox.send(low_ref, low_out)
        heads = dot_plain(low, weight_ref[...]).T.astype(jnp.bfloat16)
        for group in range(groups):
            for seq in range(batches):
                head_ref[group * batches + seq] = heads[
                    group * depth : (group + 1) * depth, seq * span : (seq + 1) * span
                ]
        outbox.send(head_ref, head_out)
        outbox.finish()

    shapes = [
        ((batches, span // 2, width), jnp.float32),
        ((rows, width), jnp.bfloat16),
        ((groups * batches, depth, span), jnp.bfloat16),
    ]
    return whole_call(
        body,
        tuple(pltpu.HBM(*shape) for shape in shapes),
        scratch=[pltpu.VMEM(*shape) for shape in shapes] + [pltpu.SemaphoreType.DMA((3,))],
        flops=2 * rows * width * groups * depth,
        nbytes=2 * width * groups * depth,
        in_specs=[SCALARS] + [VMEM] * 6,
        out_specs=(HBM,) * 3,
    )(
        indices, in_hbm(upstream), in_hbm(part_own), part_other, in_hbm(middle), in_hbm(gain_vec[None]),
        out_w,
    )


def heads_back(row_grads, weights, batches, indices, depth):
    span = row_grads.shape[2]
    rows = batches * span
    width = weights[0].shape[0]
    first = depth - 2 * HD

    def body(at_ref, grad_ref, query_ref, key_ref, value_ref, keep_ref, send_ref):
        def picked(start, stop):
            return rows_side_by_side(grad_ref, start, stop, batches)

        total = dot_plain(query_ref[...], picked(0, first))
        total += dot_plain(key_ref[...], picked(first, first + HD))
        total += dot_plain(value_ref[...], picked(first + HD, depth))
        total = total.T.astype(jnp.bfloat16)
        keep_ref[...] = own_half(total, at_ref[CORE], batches)
        send_ref[...] = own_half(total, 1 - at_ref[CORE], batches)

    columns = sum(weight.shape[1] for weight in weights)
    return whole_call(
        body,
        (pltpu.HBM((batches, span // 2, width), jnp.bfloat16),) * 2,
        flops=2 * rows * width * columns,
        nbytes=2 * width * columns,
        in_specs=[SCALARS] + [VMEM] * 4,
    )(indices, row_grads, *weights)


def input_back(
    part_own, part_other, middle_grad, section_in, gain_vec, indices, other, last=None
):
    batches, half_rows, width = middle_grad.shape

    def body(at_ref, own_ref, other_ref, grad_ref, in_ref, gain_ref, *refs):
        rows = own_half(in_ref[...], at_ref[CORE], batches).astype(jnp.float32)
        normed_grad = own_ref[...].astype(jnp.float32) + other_ref[...].astype(jnp.float32)
        _, normed, inv_scale = normalize(rows, gain_ref[...])
        down_grad = norm_back(normed_grad, normed, inv_scale, gain_ref[...])[0]
        total = grad_ref[...] + down_grad
        if last is None:
            given_ref, out_ref, low_ref = refs
            low = total.astype(jnp.bfloat16)
            low_ref[...] = jnp.where(at_ref[SECTION] == 0, given_ref[...], low)
        else:
            given_ref, last_ref, out_ref, cast_ref = refs
            total = jnp.where(at_ref[SECTION] == 0, total, given_ref[...])
            cast_ref[...] = last_ref[...].astype(jnp.float32)
        out_ref[...] = total

    shape = (batches, half_rows, width)
    outs = [pltpu.HBM(shape, jnp.float32), pltpu.HBM(shape, jnp.bfloat16)]
    if last is not None:
        outs[1] = pltpu.HBM(last.shape, jnp.float32)
    more = () if last is None else (in_hbm(last),)
    return whole_call(
        body,
        tuple(outs),
        nbytes=24 * batches * half_rows * width,
        in_specs=[SCALARS] + [VMEM] * (6 + len(more)),
    )(
        indices, in_hbm(part_own), part_other, in_hbm(middle_grad), in_hbm(section_in),
        in_hbm(gain_vec[None]), in_hbm(other), *more,
    )


ROWS = 1024


class Rows:
    def __init__(self, source, target, sems):
        self.target = target
        self.first, self.at = pl.program_id(0) == 0, pl.program_id(1)
        self.copies = [
            pltpu.make_async_copy(
                source.at[pl.ds(first, ROWS)], target.at[pl.ds(first, ROWS)], sems.at[at]
            )
            for at, first in enumerate(range(0, target.shape[0], ROWS))
        ]

        @pl.when(self.first & (self.at == 0))
        def _():
            for copy in self.copies:
                copy.start()

        for at, copy in enumerate(self.copies):

            @pl.when(self.first & (self.at == at))
            def _():
                copy.wait()

        self.place = pl.ds(pl.multiple_of(self.at * ROWS, ROWS), ROWS)

    def chunk(self):
        return self.target[self.place]

    def columns(self, ctx_at, owned):
        first = pl.multiple_of((ctx_at // 2) * 2 * owned, 2 * owned)
        pair = self.target[self.place, pl.ds(first, 2 * owned)].T
        return jnp.where(ctx_at % 2 == 0, pair[:owned], pair[owned:])


def row_scratch(rows, width):
    return [pltpu.VMEM((rows, width), jnp.bfloat16), pltpu.SemaphoreType.DMA((rows // ROWS,))]


def hidden_of_all(mlp_all, gate_w, up_w, first, steps, indices, blocks, kept=()):
    rows, width = mlp_all.shape
    hidden = gate_w.shape[1]
    owned = width // blocks
    first_part = not kept

    def body(at_ref, all_ref, gate_ref, up_ref, *refs):
        target, row_sems, slots, sems = refs[-4:]
        inner_ref, gate_f_ref, up_f_ref, *cols_ref = refs[len(kept) : -4]
        stream = Stream((gate_ref, up_ref), slots, sems, steps, first)
        fetched = Rows(all_ref, target, row_sems)
        gate_block, up_block = stream.blocks()
        low = fetched.chunk()
        inner, gate_f, up_f = hidden_factors(dot_plain(low, gate_block), dot_plain(low, up_block))
        inner_ref[...] = inner.astype(jnp.bfloat16)
        gate_f_ref[...] = gate_f.astype(jnp.bfloat16)
        up_f_ref[...] = up_f.astype(jnp.bfloat16)
        if first_part:

            @pl.when(stream.step == 0)
            def _():
                cols_ref[0][:, fetched.place] = fetched.columns(at_ref[CTX], owned)

    cols = pltpu.HBM((owned, rows), jnp.bfloat16)
    block = pl.BlockSpec((ROWS, HIDDEN), lambda step, at, *_: (at, first + step))
    return stepped_call(
        body,
        indices,
        (steps, rows // ROWS),
        [HBM] * (3 + len(kept)),
        (pltpu.HBM((rows, hidden), jnp.bfloat16),) * 3 + (cols,) * first_part,
        (block,) * 3 + (full_block(cols),) * first_part,
        row_scratch(rows, width) + weight_slots(2, width),
        4 * rows * width * HIDDEN * steps,
        2 * rows * width + (4 * width + 6 * rows) * HIDDEN * steps,
        40,
        aliases={4 + i: i for i in range(len(kept))},
    )(*map(in_hbm, (mlp_all, gate_w, up_w, *kept)))


def hidden_grads(upstream_rows, down_w, hidden_kept, indices, weights, first, steps, kept=()):
    rows, width = upstream_rows.shape
    hidden = down_w.shape[1]
    owned = hidden_kept[3].shape[0]
    chunks = rows // ROWS

    def body(
        at_ref, rows_ref, down_ref, inner_ref, gate_f_ref, up_f_ref, mlp_ref, gate_ref, up_ref, *refs
    ):
        *outs, cols_ref, target, row_sems, slots, sems = refs[len(kept) :]
        stream = Stream((down_ref,), slots, sems, steps, first)
        fetched = Rows(rows_ref, target, row_sems)
        (down_block,) = stream.blocks()

        @pl.when(stream.step == 0)
        def _():
            cols_ref[:, fetched.place] = fetched.columns(at_ref[CTX], owned)

        inner_grad = dot_plain(fetched.chunk(), down_block)
        gate_grad = (inner_grad * gate_f_ref[...].astype(jnp.float32)).astype(jnp.bfloat16)
        up_grad = (inner_grad * up_f_ref[...].astype(jnp.float32)).astype(jnp.bfloat16)
        mlp_cols = mlp_ref[:, fetched.place]
        pieces = (
            dot_plain(mlp_cols, gate_grad),
            dot_plain(mlp_cols, up_grad),
            dot_plain(cols_ref[:, fetched.place], inner_ref[...]),
        )

        @pl.when(stream.begins)
        def _():
            for out, piece in zip(outs, pieces):
                out[...] = piece

        @pl.when(jnp.logical_not(stream.begins))
        def _():
            for out, piece in zip(outs, pieces):
                out[...] += piece

        @pl.when(fetched.at == chunks - 1)
        def _():
            products = outs[0][...] * gate_ref[...].astype(jnp.float32)
            products += outs[1][...] * up_ref[...].astype(jnp.float32)
            products = jnp.sum(products, axis=1, keepdims=True)
            outs[3][...] = jnp.where(stream.step == 0, products, outs[3][...] + products)

    owned_block = pl.BlockSpec((owned, HIDDEN), lambda step, at, at_ref: (at_ref[CTX], first + step))
    out_block = pl.BlockSpec((owned, HIDDEN), lambda step, at, *_: (0, first + step))
    row_block = pl.BlockSpec((ROWS, HIDDEN), lambda step, at, *_: (at, first + step))
    sums = pltpu.HBM((owned, 1), jnp.float32)
    return stepped_call(
        body,
        indices,
        (steps, chunks),
        [HBM] * 2
        + [row_block] * 3
        + [full_block(hidden_kept[3])]
        + [owned_block] * 2
        + [HBM] * len(kept),
        (pltpu.HBM((owned, hidden), jnp.float32),) * 3 + (sums,),
        (out_block,) * 3 + (full_block(sums),),
        [pltpu.VMEM((owned, rows), jnp.bfloat16)] + row_scratch(rows, width) + weight_slots(1, width),
        (2 * rows * width + 6 * owned * rows) * HIDDEN * steps,
        2 * rows * width + (2 * width + 6 * rows) * HIDDEN * steps,
        40,
        aliases={9 + i: i for i in range(len(kept))},
    )(*map(in_hbm, (upstream_rows, down_w, *hidden_kept, *weights, *kept)))


def taken(place, groups, targets, sems):
    for at, (sources, target) in enumerate(zip(groups, targets)):
        for number, source in enumerate(sources):

            @pl.when(place == number)
            def _():
                pltpu.make_async_copy(source, target, sems.at[at]).start()

    for at, (sources, target) in enumerate(zip(groups, targets)):
        pltpu.make_async_copy(sources[0], target, sems.at[at]).wait()


def split_owners(total, owned, seq_at, keep_ref, send_ref):
    pairs = keep_ref.shape[0]
    for pair in range(pairs):
        lower, upper = (total(2 * pair * owned + half * owned, owned) for half in range(2))
        keep_ref[pair] = jnp.where(seq_at == 0, lower, upper)
        send_ref[pair] = jnp.where(seq_at == 0, upper, lower)


def head_weight_grads(head_grads, attn_rows, indices):
    blocks, depth, span = head_grads[0].shape
    rows, width = attn_rows[0].shape
    owned = width // blocks

    def body(
        at_ref, grad_0, grad_1, rows_0, rows_1, out_ref, grad_ref, rows_ref, sems
    ):
        groups = ((grad_0, grad_1), (rows_0, rows_1))
        taken(at_ref[SECTION], groups, (grad_ref, rows_ref), sems)
        total = dot_plain(side_by_side(grad_ref, 0, depth), rows_ref[...]).T.astype(jnp.bfloat16)
        for owner in range(blocks):
            out_ref[owner, :depth] = grad_ref[owner]
            own = slice(owner * owned, (owner + 1) * owned)
            for at in range(depth // span):
                place = slice(depth + at * owned, depth + (at + 1) * owned)
                out_ref[owner, place] = total[own, at * span : (at + 1) * span]

    return whole_call(
        body,
        pltpu.HBM((blocks, depth + depth // span * owned, span), jnp.bfloat16),
        scratch=[
            pltpu.VMEM(head_grads[0].shape, jnp.bfloat16),
            pltpu.VMEM((rows, width), jnp.bfloat16),
            pltpu.SemaphoreType.DMA((2,)),
        ],
        flops=2 * rows * width * depth,
        nbytes=2 * rows * width,
        in_specs=[SCALARS] + [HBM] * 4,
    )(indices, *map(in_hbm, (*head_grads, *attn_rows)))


def out_weight_grads(middle_lows, mixed, indices, blocks):
    rows, width = middle_lows[0].shape
    heads = mixed[0].shape[1]
    owned = width // blocks

    def body(
        at_ref, low_0, low_1, mixed_0, mixed_1, keep_ref, send_ref, low_ref, mixed_ref, sems
    ):
        groups = ((low_0, low_1), (mixed_0, mixed_1))
        taken(at_ref[SECTION], groups, (low_ref, mixed_ref), sems)
        total = dot_plain(low_ref[...].T, mixed_ref[...]).astype(jnp.bfloat16)
        split_owners(
            lambda first, size: total[first : first + size], owned, at_ref[SEQ], keep_ref, send_ref
        )

    half = pltpu.HBM((blocks // 2, owned, heads), jnp.bfloat16)
    return whole_call(
        body,
        (half, half),
        scratch=[
            pltpu.VMEM((rows, width), jnp.bfloat16),
            pltpu.VMEM((rows, heads), jnp.bfloat16),
            pltpu.SemaphoreType.DMA((2,)),
        ],
        flops=2 * rows * width * heads,
        nbytes=2 * width * heads,
        grant=18,
        in_specs=[SCALARS] + [HBM] * 4,
    )(indices, *map(in_hbm, (*middle_lows, *mixed)))


def own_weight_grads(arrived, weights, more_sums, indices, depth):
    blocks, size, span = arrived.shape
    owned = (size - depth) * span // depth
    batches = 2
    first = depth - 2 * HD

    def body(
        _, in_ref, query_ref, key_ref, value_ref, first_ref, second_ref,
        query_out, key_out, value_out, sum_out,
    ):
        totals = [
            sum(
                jnp.concatenate(
                    [
                        in_ref[block + seq, depth + at * owned : depth + (at + 1) * owned]
                        for at in range(depth // span)
                    ],
                    axis=1,
                ).astype(jnp.float32)
                for seq in range(batches)
            )
            for block in range(0, blocks, batches)
        ]
        products = 0.0
        for ref, out, start, stop in (
            (query_ref, query_out, 0, first),
            (key_ref, key_out, first, first + HD),
            (value_ref, value_out, first + HD, depth),
        ):
            grad = jnp.concatenate([total[:, start:stop] for total in totals], axis=1)
            out[...] = grad
            products += jnp.sum(grad * ref[...].astype(jnp.float32), axis=1, keepdims=True)
        sums = (products, first_ref[...] + second_ref[...])
        for row, column in enumerate(sums):
            sum_out[row : row + 1] = jnp.broadcast_to(column, (owned, 128)).T[:1]

    outs = [pltpu.HBM((owned, weight.shape[1]), jnp.float32) for weight in weights]
    outs.append(pltpu.HBM((2, owned), jnp.float32))
    return stepped_call(
        body,
        indices,
        (1,),
        [full_block(arrived)]
        + [
            pl.BlockSpec((owned, weight.shape[1]), lambda step, at_ref: (at_ref[CTX], 0))
            for weight in weights
        ]
        + [full_block(more_sums[0])] * 2,
        outs,
        [full_block(out) for out in outs],
        [],
        0,
        6 * blocks * depth * owned,
        18,
    )(arrived, *map(in_hbm, weights), *more_sums)


def swap_blocks(pieces, members=None):
    return lax.all_to_all(
        pieces, "ctx", split_axis=0, concat_axis=0, axis_index_groups=members
    )


def other_core(array):
    return lax.ppermute(array, "tp", [(0, 1), (1, 0)])


def tied(*arrays):
    return lax.optimization_barrier(arrays)


def on_device(
    inputs, cotangent, norm_attn, w_query, w_key, w_value, w_out, norm_mlp, w_gate, w_up, w_down
):
    params = tuple(
        weight[0]
        for weight in (norm_attn, w_query, w_key, w_value, w_out, norm_mlp, w_gate, w_up, w_down)
    )
    gain_attn, query_w, key_w, value_w, out_w, gain_mlp, gate_w, up_w, down_w = params
    batches, local_rows, width = inputs.shape
    span_rows = local_rows * lax.axis_size("tp")
    blocks = lax.axis_size("ctx")
    seq_len = span_rows * blocks
    half_rows = span_rows // 2
    halves = 2 * blocks
    groups = key_w.shape[1] // HD
    repeat = query_w.shape[1] // key_w.shape[1]
    section_at = lax.axis_index("pipe")
    sections = lax.axis_size("pipe")
    ctx_at = lax.axis_index("ctx")
    tp_at = lax.axis_index("tp")
    seq_at = ctx_at % batches
    rows = batches * span_rows
    owned = width // blocks
    indices = jnp.stack([tp_at, seq_at, ctx_at, section_at])
    own_pos = place_rows(
        ctx_at * span_rows + jnp.arange(span_rows, dtype=jnp.int32), half_rows, halves
    )
    cosine, sine_tab = (
        jnp.tile(tab[:, : HD // 2].T, (1, batches)) for tab in rotary_tables(own_pos)
    )
    all_cosine, all_sine = (tab[:, : HD // 2].T for tab in rotary_tables(jnp.arange(seq_len)))
    neighbours = [(i, i ^ 1) for i in range(blocks)]
    same_x = [list(range(x, blocks, 2)) for x in range(2)]

    def tp_rows(part):
        return lax.all_gather(part, "tp", axis=1, tiled=True).reshape(rows, width)

    def own_part(full):
        full = full.reshape(batches, span_rows, width)
        return lax.dynamic_slice_in_dim(full, tp_at * local_rows, local_rows, 1)

    def here(per_section):
        picked = per_section[0]
        for section, value in enumerate(per_section[1:], 1):
            picked = jnp.where(section_at == section, value, picked)
        return picked

    def rows_of_all(part):
        return lax.all_gather(part.reshape(-1, width), ("ctx", "tp"), axis=0, tiled=True)

    def part_of_sequence(mine, theirs):
        pairs = [(2 * i + i % 2, 2 * (i ^ 1) + i % 2) for i in range(blocks)]
        theirs = lax.ppermute(theirs, ("ctx", "tp"), pairs)
        return jnp.where(tp_at == seq_at, mine, theirs)

    def rows_of_sequence(part):
        members = [
            [2 * (pair * batches + seq) + core for pair in range(groups) for core in range(2)]
            for seq in range(batches)
        ]
        return lax.all_gather(
            part, ("ctx", "tp"), axis=0, tiled=True, axis_index_groups=members
        )

    def added(keep, send):
        arrived = lax.ppermute(send, "ctx", neighbours)
        return (keep.astype(jnp.float32) + arrived.astype(jnp.float32)).astype(jnp.bfloat16)

    def owned_gain(gain_vec):
        return lax.dynamic_slice_in_dim(gain_vec, ctx_at * owned, owned, 0)

    states, attn_rows, mlp_parts = [], [], []
    arrived = inputs
    weights = (key_w, value_w, out_w)
    hidden_weights = (gate_w, up_w, down_w)
    held = tuple(map(in_hbm, weights))
    for section in range(sections):
        section_in = tp_rows(arrived)
        mine, theirs, pieces = project_heads(
            section_in, gain_attn, (in_hbm(query_w), *held[:2]), cosine, sine_tab, indices
        )
        attn_part = part_of_sequence(mine, theirs)
        head_qkv, attn_part = tied(swap_blocks(pieces), attn_part)
        if section == 0:
            cotangent_rows, *loaded = tied(cotangent, mine, *weights)
            cotangent_rows = tp_rows(cotangent_rows)
            held = tuple(map(in_vmem, load_weights(loaded[1:])))
            head_qkv, cotangent_rows = tied(head_qkv, cotangent_rows)
        head_mixed, log_total = attend_heads(head_qkv, repeat)
        if section == 1:
            head_mixed, attn_rows[0] = tied(head_mixed, attn_rows[0])
        mixed, attn_own = project_out(swap_blocks(head_mixed), held[2], batches)
        if section == 0:
            attn_own, attn_part = tied(attn_own, attn_part)
            attn_rows.append(rows_of_sequence(attn_part))
        middle, mlp_part, gate_f, up_f, part_own, part_sent = feed_forward(
            section_in, attn_own, other_core(attn_own), gain_mlp, hidden_weights, batches, indices
        )
        mlp_parts.append(mlp_part)
        if section == 1:
            mlp_part, part_sent = tied(here(mlp_parts), part_sent)
            mlp_rows = rows_of_all(mlp_part)
        total = part_own.astype(jnp.float32) + other_core(part_sent).astype(jnp.float32)
        outgoing = (own_part(middle) + total).astype(jnp.bfloat16)
        states.append((section_in, head_qkv, log_total, mixed, middle, gate_f, up_f, outgoing))
        if section == 0:
            arrived = shifted(outgoing, "pipe", 1)
    section_out = here([state[-1] for state in states])

    def recompute(first, steps, after, kept=()):
        later_rows, _ = tied(mlp_rows, after)
        return hidden_of_all(later_rows, gate_w, up_w, first, steps, indices, blocks, kept)

    all_steps = gate_w.shape[1] // HIDDEN
    depth = (repeat + 2) * HD
    middle_lows, head_parts = [None] * 2, [None] * 2
    for section in (1, 0):
        section_in, head_qkv, log_total, mixed, middle, gate_f, up_f, _ = states[section]
        upstream = cotangent_rows if section == 1 else tp_rows(arrived)
        if section == 0:
            upstream, arrived = tied(upstream, arrived)
            upstream_rows = rows_of_all(arrived)
        part_own = feed_forward_back(upstream, gate_f, up_f, hidden_weights)
        middle_grad, middle_lows[section], mixed_grad = middle_back(
            upstream, part_own, other_core(part_own), middle, gain_mlp, held[2], groups, batches,
            indices,
        )
        head_grad = swap_blocks(mixed_grad)
        if section == 0:
            hidden_kept = recompute(1, all_steps - 2, mixed_grad, hidden_kept)
            head_grad, *hidden_kept = tied(head_grad, *hidden_kept)
        head_parts[section] = head_grads = attend_heads_back(
            head_qkv, head_grad, log_total, all_cosine, all_sine, repeat
        )
        if section == 1:
            row_grads, section_out = tied(swap_blocks(head_grads), section_out)
            attn_part, _ = tied(attn_part, head_grads)
            attn_rows.append(rows_of_sequence(attn_part))
        else:
            pieces = head_weight_grads(head_parts, attn_rows, indices)
            row_grads = swap_blocks(pieces)
            middle_lows[0], _ = tied(middle_lows[0], pieces)
            out_own, out_sent = out_weight_grads(
                middle_lows, [state[3] for state in states], indices, blocks
            )
            hidden_kept = (*recompute(all_steps - 1, 1, out_own, hidden_kept), mlp_cols)
            first_steps = all_steps // 2
            *hidden_out, early_sums = hidden_grads(
                upstream_rows, down_w, hidden_kept, indices, (gate_w, up_w), 0, first_steps
            )
            out_own, *hidden_out = tied(out_own, *hidden_out)
            out_sum, *hidden_out = tied(added(out_own, out_sent), *hidden_out)
            grad_out = lax.psum_scatter(
                out_sum, "ctx", scatter_dimension=0, axis_index_groups=same_x
            )
            *hidden_out, late_sums = hidden_grads(
                upstream_rows, down_w, hidden_kept, indices, (gate_w, up_w), first_steps,
                all_steps - first_steps, hidden_out,
            )
            row_grads, *hidden_out = tied(row_grads, *hidden_out)
        part_own, part_sent = heads_back(
            row_grads, (in_hbm(query_w), *held[:2]), batches, indices, depth
        )
        part_other = other_core(part_sent)
        if section == 0:
            input_grads, grad_out = input_back(
                part_own, part_other, middle_grad, section_in, gain_attn, indices, input_grads, grad_out
            )
        else:
            input_grads, input_low = input_back(
                part_own, part_other, middle_grad, section_in, gain_attn, indices, cotangent
            )
            arrived = lax.ppermute(input_low, "pipe", [(0, 1), (1, 0)])
            *hidden_kept, mlp_cols = recompute(0, 1, input_low)
            arrived, *hidden_kept = tied(arrived, *hidden_kept)
    grad_query, grad_key, grad_value, gains = own_weight_grads(
        row_grads, (query_w, key_w, value_w), (early_sums, late_sums), indices, depth
    )
    grad_gate, grad_up, grad_down = hidden_out
    gains = jnp.sum(lax.all_gather(gains, "tp", axis=0), axis=0)
    gains = gains / jnp.stack([owned_gain(gain_attn), owned_gain(gain_mlp)])
    outs = (
        section_out,
        input_grads,
        gains[0],
        grad_query,
        grad_key,
        grad_value,
        grad_out,
        gains[1],
        grad_gate,
        grad_up,
        grad_down,
    )
    return tuple(out[None] for out in outs)


def solution(mesh):
    placed = (
        P(None, ("ctx", "tp"), None),
        P(None, ("ctx", "tp"), None),
        P("pipe", None),
        P("pipe", None, "tp"),
        P("pipe", None, "tp"),
        P("pipe", None, "tp"),
        P("pipe", None, "tp"),
        P("pipe", None),
        P("pipe", None, "tp"),
        P("pipe", None, "tp"),
        P("pipe", None, "tp"),
    )

    def chosen(*arrays):
        batches, groups = arrays[0].shape[0], arrays[4].shape[-1] // HD
        alike = batches == 2 and mesh.shape["ctx"] == batches * groups
        alike = alike and mesh.shape["tp"] == 2 and mesh.shape["pipe"] == 2
        return (on_device if alike else on_device_wide)(*arrays)

    return jax.shard_map(
        chosen,
        mesh=mesh,
        in_specs=placed,
        out_specs=(
            P("pipe", None, ("ctx", "tp"), None),
            P("pipe", None, ("ctx", "tp"), None),
            P("pipe", "ctx"),
            P("pipe", "ctx", "tp"),
            P("pipe", "ctx", "tp"),
            P("pipe", "ctx", "tp"),
            P("pipe", "ctx", "tp"),
            P("pipe", "ctx"),
            P("pipe", "ctx", "tp"),
            P("pipe", "ctx", "tp"),
            P("pipe", "ctx", "tp"),
        ),
        check_vma=False,
    )
```
